32 devices in a mesh: region: 8 (over y, x, core), pos: 4 (over z).
Axes of the slice: x: 2, y: 2, z: 4, core: 2. Of those that a mesh axis runs over, the one named last changes fastest.
Arguments:
- object_tiles: float32 [128, 2, 2, 128, 128], P('region'), may hold values from -4 to 4
- probe: float32 [4, 2, 256, 256], replicated, may hold values from -3 to 3
- fresnel_phase: float32 [256, 256], replicated, may hold values from -3.140625 to 3.140625
- patterns: float32 [8, 4, 2, 256, 256], P('region', 'pos'), may hold values from 0 to 4
- row_offsets: int32 [8, 4, 2], P('region', 'pos'), may hold values from 0 to 1792, as said below
- col_offsets: int32 [8, 4, 2], P('region', 'pos'), may hold values from 0 to 768
- counts: int32 [8, 4], P('region', 'pos'), may hold values from 1 to 2, as said below
Outputs:
- new_object: float32 [128, 2, 2, 128, 128], P('region')
The draws below stay inside these ranges and needn't reach their ends.
Inputs may be any that keep to these rules, and one draw needn't show every extreme that they name: A device's live positions are its first counts slots; the other slots of its position arrays are ignored. Some device holds 2 live positions. `row_offsets`: every slot of region index r starts at a row from r * 2 * 128 to r * 2 * 128 + 2 * 128 - 1, and never after row 1792.
All inputs are finite; a program needn't handle non-finite values.
Results may differ from the reference program's by a relative error of at most 0.0095.
Values sent between devices are 32-bit elements; how exact they have to be, the bound alone decides.
A program may use at most 128 MiB of HBM per device.

```python
import math
import jax
import jax.numpy as jnp
from jax import lax

PIX = 256
MODES = 4
S = 2
TILE = 128
TGX = 8
BR = 2
POS_DEV = 2
NT = 128
TGY = 16
OH = 2048
OW = 1024
N_REGION = 8
N_POS = 4


def draw_counts(key, part):
    first_key, second_key = jax.random.split(key)
    heavy_rank = jax.random.randint(first_key, (N_REGION, N_POS), 0, 8) == 0
    chosen = jax.random.randint(second_key, (), 0, N_REGION * N_POS)
    places = jnp.arange(N_REGION * N_POS, dtype=jnp.int32).reshape(N_REGION, N_POS)
    return jnp.where(heavy_rank | (places == chosen), POS_DEV, 1).astype(jnp.int32)


def draw_row_offsets(key, part):
    band_rows = BR * TILE
    band_start = jnp.arange(N_REGION, dtype=jnp.int32)[:, None, None] * band_rows
    within = jax.random.randint(jax.random.fold_in(key, 11), (N_REGION, N_POS, POS_DEV), 0, band_rows)
    within = within.at[0, 0, 0].set(0)
    return jnp.minimum(band_start + within, OH - PIX).astype(jnp.int32)


def touch_ends(drawn, stream_key, low, largest):
    spot = [jax.random.randint(jax.random.fold_in(stream_key, axis), (), 0, length) for axis, length in enumerate(drawn.shape)]
    main_axis = drawn.shape.index(max(drawn.shape))
    beside = spot[:main_axis] + [(spot[main_axis] + 1) % drawn.shape[main_axis]] + spot[main_axis + 1:]
    return drawn.at[tuple(spot)].set(low).at[tuple(beside)].set(largest)


def level_of(own_key, dims, pieces, low, top_value):
    factor_of = 1.0
    for dim, shards_of in pieces:
        draws = jax.random.uniform(jax.random.fold_in(jax.random.fold_in(own_key, 6), dim), (shards_of,), jnp.float32, low / len(pieces), top_value / len(pieces))
        factor_of = factor_of * jnp.repeat(jnp.exp(draws), dims[dim] // shards_of).reshape((-1,) + (1,) * (len(dims) - 1 - dim))
    return factor_of


def scatter_about(key, extent, deviation, limit, cuts=(), kind=jnp.bfloat16):
    array = deviation * jax.random.normal(key, extent, jnp.float32)
    if cuts:
        array = array * level_of(key, extent, cuts, -0.22, 0.18)
    return jnp.clip(array, -limit, limit).astype(kind)


def setup_inputs(seed: int = 0) -> dict:
    key_of = jax.random.split(jax.random.key(seed), 8)
    object_tiles = scatter_about(key_of[0], (NT, S, 2, TILE, TILE), 0.7, 4.0, ((0, 8),), jnp.float32)
    probe = scatter_about(key_of[1], (MODES, 2, PIX, PIX), 0.5, 3.0, (), jnp.float32)
    fresnel_phase = jnp.clip(jax.random.uniform(key_of[2], (PIX, PIX), jnp.float32, -3.140625, 3.140625), -3.140625, 3.140625)
    patterns = jnp.clip(4.0 * jax.random.uniform(key_of[3], (N_REGION, N_POS, POS_DEV, PIX, PIX), jnp.float32) ** level_of(key_of[3], (N_REGION, N_POS, POS_DEV, PIX, PIX), ((0, 8), (1, 4)), -0.2, 0.2), 0.0, 4.0)
    row_offsets = draw_row_offsets(jax.random.fold_in(key_of[7], 71), 0)
    col_offsets = touch_ends(jax.random.randint(key_of[5], (N_REGION, N_POS, POS_DEV), 0, OW - PIX + 1), jax.random.fold_in(key_of[5], 1), 0, OW - PIX).astype(jnp.int32)
    counts = draw_counts(jax.random.fold_in(key_of[7], 71), 0)
    return dict(object_tiles=object_tiles, probe=probe, fresnel_phase=fresnel_phase, patterns=patterns, row_offsets=row_offsets, col_offsets=col_offsets, counts=counts)


step_size = 0.05

def make_tables(length):
    counter = jnp.arange(length, dtype=jnp.int32)
    product = counter[:, None] * counter[None, :] % length
    angles = product.astype(jnp.float32) * jnp.float32(2.0 * math.pi / length)
    factor = jnp.float32(1.0 / math.sqrt(length))
    return ((jnp.cos(angles) * factor).astype(jnp.bfloat16), (jnp.sin(angles) * factor).astype(jnp.bfloat16))

def left_product(matrix, field):
    return jnp.einsum('jk,mkl->mjl', matrix.astype(jnp.float32), field.astype(jnp.float32), precision=lax.Precision.HIGHEST)

def right_product(field, matrix):
    return jnp.einsum('mjk,kl->mjl', field.astype(jnp.float32), matrix.astype(jnp.float32), precision=lax.Precision.HIGHEST)

def transform(field_re, field_im, direction, cos_table, sin_table):
    field_re = field_re.astype(jnp.bfloat16)
    field_im = field_im.astype(jnp.bfloat16)
    upper_re = left_product(cos_table, field_re) - direction * left_product(sin_table, field_im)
    upper_im = left_product(cos_table, field_im) + direction * left_product(sin_table, field_re)
    upper_re = upper_re.astype(jnp.bfloat16)
    upper_im = upper_im.astype(jnp.bfloat16)
    result_re = right_product(upper_re, cos_table) - direction * right_product(upper_im, sin_table)
    result_im = right_product(upper_im, cos_table) + direction * right_product(upper_re, sin_table)
    return (result_re, result_im)

def complex_product(left_re, left_im, right_re, right_im):
    return (left_re * right_re - left_im * right_im, left_re * right_im + left_im * right_re)

def conj_product(left_re, left_im, right_re, right_im):
    return (left_re * right_re + left_im * right_im, left_re * right_im - left_im * right_re)

def position_gradient(patch, probe, wave_re, wave_im, measured, cos_table, sin_table):
    slice_count = patch.shape[0]
    field_re = probe[:, 0]
    field_im = probe[:, 1]
    incoming = []
    for layer_index in range(slice_count):
        incoming.append((field_re, field_im))
        exit_re, exit_im = complex_product(field_re, field_im, patch[layer_index, 0], patch[layer_index, 1])
        exit_re = exit_re.astype(jnp.bfloat16)
        exit_im = exit_im.astype(jnp.bfloat16)
        if layer_index + 1 < slice_count:
            spec_re, spec_im = transform(exit_re, exit_im, -1.0, cos_table, sin_table)
            spec_re, spec_im = complex_product(wave_re, wave_im, spec_re, spec_im)
            field_re, field_im = transform(spec_re.astype(jnp.bfloat16), spec_im.astype(jnp.bfloat16), 1.0, cos_table, sin_table)
    far_re, far_im = transform(exit_re, exit_im, -1.0, cos_table, sin_table)
    intensity = lax.optimization_barrier(jnp.sum(far_re * far_re + far_im * far_im, axis=0))
    misfit = intensity - measured
    back_re, back_im = transform((misfit * far_re).astype(jnp.bfloat16), (misfit * far_im).astype(jnp.bfloat16), 1.0, cos_table, sin_table)
    results = [None] * slice_count
    for layer_index in reversed(range(slice_count)):
        incident_re, incident_im = incoming[layer_index]
        grad_re, grad_im = conj_product(incident_re, incident_im, back_re, back_im)
        results[layer_index] = jnp.stack([lax.optimization_barrier(jnp.sum(grad_re, axis=0)), lax.optimization_barrier(jnp.sum(grad_im, axis=0))])
        if layer_index > 0:
            prior_re, prior_im = conj_product(patch[layer_index, 0], patch[layer_index, 1], back_re, back_im)
            spec_re, spec_im = transform(prior_re.astype(jnp.bfloat16), prior_im.astype(jnp.bfloat16), -1.0, cos_table, sin_table)
            spec_re, spec_im = conj_product(wave_re, wave_im, spec_re, spec_im)
            back_re, back_im = transform(spec_re.astype(jnp.bfloat16), spec_im.astype(jnp.bfloat16), 1.0, cos_table, sin_table)
    return jnp.stack(results)

def reference(object_tiles, probe, fresnel_phase, patterns, row_offsets, col_offsets, counts):
    image = object_tiles.reshape(TGY, TGX, S, 2, TILE, TILE).transpose(2, 3, 0, 4, 1, 5).reshape(S, 2, OH, OW)
    cos_table, sin_table = make_tables(PIX)
    wave_re = jnp.cos(fresnel_phase)
    wave_im = jnp.sin(fresnel_phase)
    measured = patterns.reshape(-1, PIX, PIX)
    row_start = row_offsets.reshape(-1).astype(jnp.int32)
    col_start = col_offsets.reshape(-1).astype(jnp.int32)
    slot_number = jnp.arange(POS_DEV, dtype=jnp.int32)
    alive = (slot_number[None, None, :] < counts[:, :, None]).reshape(-1)
    zero_index = jnp.int32(0)

    def visit(gradient, items):
        pattern, first_row, first_col, flag = items
        corner = (zero_index, zero_index, first_row, first_col)

        def compute(current):
            patch = lax.dynamic_slice(image, corner, (S, 2, PIX, PIX))
            term = position_gradient(patch, probe, wave_re, wave_im, pattern, cos_table, sin_table)
            former = lax.dynamic_slice(current, corner, (S, 2, PIX, PIX))
            return lax.dynamic_update_slice(current, former + term, corner)

        def unchanged(current):
            return current
        return (lax.cond(flag, compute, unchanged, gradient), None)
    gradient, _ = lax.scan(visit, jnp.zeros((S, 2, OH, OW), jnp.float32), (measured, row_start, col_start, alive))
    tile_gradient = gradient.reshape(S, 2, TGY, TILE, TGX, TILE).transpose(2, 4, 0, 1, 3, 5).reshape(NT, S, 2, TILE, TILE)
    return object_tiles - step_size * tile_gradient
```

```python
import functools
import math

import jax
import jax.numpy as jnp
from jax import lax
from jax.experimental import pallas as pl
from jax.experimental.pallas import tpu as pltpu
from jax.sharding import PartitionSpec as P

TGX = 8
LANES = 128

step_size = 0.05


def shifted(shard, axis, by):
    count = lax.axis_size(axis)
    pairs = [(i, i + by) for i in range(count) if 0 <= i + by < count]
    return lax.ppermute(shard, axis, pairs)


def rotated(shard, axis, by):
    count = lax.axis_size(axis)
    return lax.ppermute(shard, axis, [(i, (i + by) % count) for i in range(count)])


def make_tables(length):
    counter = jnp.arange(length, dtype=jnp.int32)
    product = counter[:, None] * counter[None, :] % length
    angles = product.astype(jnp.float32) * jnp.float32(2.0 * math.pi / length)
    factor = jnp.float32(1.0 / math.sqrt(length))
    return (
        (jnp.cos(angles) * factor).astype(jnp.bfloat16),
        (jnp.sin(angles) * factor).astype(jnp.bfloat16),
    )


def make_matrices(length):
    cos_table, sin_table = make_tables(length)
    plus = jnp.concatenate(
        [
            jnp.concatenate([cos_table, -sin_table], axis=1),
            jnp.concatenate([sin_table, cos_table], axis=1),
        ],
        axis=0,
    )
    minus = jnp.concatenate(
        [
            jnp.concatenate([cos_table, sin_table], axis=1),
            jnp.concatenate([-sin_table, cos_table], axis=1),
        ],
        axis=0,
    )
    return jnp.stack([plus, minus])


def full_spec():
    return pl.BlockSpec(memory_space=pltpu.VMEM)


def scalar_spec():
    return pl.BlockSpec(memory_space=pltpu.SMEM)


def store_columns(tiles_ref, base, component, column, write):
    first = column // LANES
    shift = column % LANES
    back = (LANES - shift) % LANES
    third = jnp.minimum(first + 2, TGX - 1)
    left = pltpu.roll(tiles_ref[base + first, component], back, 1)
    middle = pltpu.roll(tiles_ref[base + first + 1, component], back, 1)
    right = pltpu.roll(tiles_ref[base + third, component], back, 1)
    lane = lax.broadcasted_iota(jnp.int32, left.shape, 1)
    keep = lane < LANES - shift
    write(0, jnp.where(keep, left, middle))
    write(1, jnp.where(keep, middle, right))


def window_kernel(column_ref, tiles_ref, out_ref):
    slots = out_ref.shape[0]
    components = tiles_ref.shape[1]
    side = tiles_ref.shape[2]
    rows = tiles_ref.shape[0] // TGX
    for slot in range(slots):
        column = column_ref[slot]

        def body(component, carry):
            for row in range(rows):

                def write(half, value):
                    out_ref[
                        slot, component, row * side : (row + 1) * side, half * LANES : (half + 1) * LANES
                    ] = value

                store_columns(tiles_ref, row * TGX, component, column, write)
            return carry

        lax.fori_loop(0, components, body, 0)


def column_windows(columns, tiles, pixels):
    band = tiles.shape[0] // TGX * tiles.shape[2]
    return pl.pallas_call(
        window_kernel,
        out_shape=jax.ShapeDtypeStruct((columns.shape[0], tiles.shape[1], band, pixels), jnp.float32),
        in_specs=[scalar_spec(), full_spec()],
        out_specs=full_spec(),
        compiler_params=pltpu.CompilerParams(vmem_limit_bytes=32 * 1024 * 1024),
    )(columns, tiles)


def position_kernel(
    place_ref,
    tiles_ref,
    halo_ref,
    probe_ref,
    wave_ref,
    measured_ref,
    matrix_ref,
    out_ref,
    canvas,
    patch,
    field,
    far,
    intensity,
):
    row = place_ref[0]
    column = place_ref[1]
    live = place_ref[2]
    components, pixels = patch.shape[0], patch.shape[1]
    modes = probe_ref.shape[0]
    side = tiles_ref.shape[2]
    band_tiles = tiles_ref.shape[0] // TGX
    band_rows = band_tiles * side
    plus, minus = 0, 1

    def fill(component, carry):
        for tile_row in range(band_tiles):

            def write(half, value):
                canvas[component, half, tile_row * side : (tile_row + 1) * side, :] = value

            store_columns(tiles_ref, tile_row * TGX, component, column, write)
        for half in range(pixels // LANES):
            lanes = slice(half * LANES, (half + 1) * LANES)
            canvas[component, half, band_rows:, :] = halo_ref[component, :, lanes]
            patch[component, :, lanes] = canvas[component, half, pl.ds(row, pixels), :]
        return carry

    lax.fori_loop(0, components, fill, 0)

    def transform(real, imag, left, right):
        stacked = jnp.concatenate([real, imag], axis=0).astype(jnp.bfloat16)
        upper = jnp.dot(matrix_ref[left], stacked, preferred_element_type=jnp.float32)
        upper = upper.astype(jnp.bfloat16)
        upper = jnp.concatenate([upper[:pixels], upper[pixels:]], axis=1)
        return jnp.dot(upper, matrix_ref[right], preferred_element_type=jnp.float32)

    def forward_transform(real, imag):
        return transform(real, imag, minus, plus)

    def inverse_transform(real, imag):
        return transform(real, imag, plus, minus)

    intensity[...] = jnp.zeros_like(intensity)

    def forward(mode, carry):
        field_re, field_im = probe_ref[mode, 0], probe_ref[mode, 1]
        spec = forward_transform(
            field_re * patch[0] - field_im * patch[1],
            field_re * patch[1] + field_im * patch[0],
        )
        spec_re, spec_im = spec[:, :pixels], spec[:, pixels:]
        moved = inverse_transform(
            wave_ref[0] * spec_re - wave_ref[1] * spec_im,
            wave_ref[0] * spec_im + wave_ref[1] * spec_re,
        )
        field[mode] = moved
        field_re, field_im = moved[:, :pixels], moved[:, pixels:]
        psi = forward_transform(
            field_re * patch[2] - field_im * patch[3],
            field_re * patch[3] + field_im * patch[2],
        )
        far[mode] = psi
        psi_re, psi_im = psi[:, :pixels], psi[:, pixels:]
        intensity[...] += psi_re * psi_re + psi_im * psi_im
        return carry

    lax.fori_loop(0, modes, forward, 0, unroll=2)

    intensity[...] -= measured_ref[...]
    out_ref[...] = jnp.zeros_like(out_ref)

    def backward(mode, carry):
        misfit = intensity[...]
        psi = far[mode]
        back = inverse_transform(misfit * psi[:, :pixels], misfit * psi[:, pixels:])
        back_re, back_im = back[:, :pixels], back[:, pixels:]
        field_re, field_im = field[mode, :, :pixels], field[mode, :, pixels:]
        out_ref[2] += field_re * back_re + field_im * back_im
        out_ref[3] += field_re * back_im - field_im * back_re
        spec = forward_transform(
            patch[2] * back_re + patch[3] * back_im,
            patch[2] * back_im - patch[3] * back_re,
        )
        spec_re, spec_im = spec[:, :pixels], spec[:, pixels:]
        back = inverse_transform(
            wave_ref[0] * spec_re + wave_ref[1] * spec_im,
            wave_ref[0] * spec_im - wave_ref[1] * spec_re,
        )
        back_re, back_im = back[:, :pixels], back[:, pixels:]
        field_re, field_im = probe_ref[mode, 0], probe_ref[mode, 1]
        out_ref[0] += field_re * back_re + field_im * back_im
        out_ref[1] += field_re * back_im - field_im * back_re
        return carry

    lax.fori_loop(0, modes, backward, 0, unroll=2)

    @pl.when(live == 0)
    def _():
        out_ref[...] = jnp.zeros_like(out_ref)


def position_gradient(place, tiles, halo, probe, wave, measured, matrices):
    components = tiles.shape[1]
    modes, _, pixels, _ = probe.shape
    band_rows = tiles.shape[0] // TGX * tiles.shape[2]
    products = 6 * modes * 2 * 2 * (2 * pixels) ** 2 * pixels
    return pl.pallas_call(
        position_kernel,
        out_shape=jax.ShapeDtypeStruct((components, pixels, pixels), jnp.float32),
        in_specs=[scalar_spec()] + [full_spec()] * 6,
        out_specs=full_spec(),
        scratch_shapes=[
            pltpu.VMEM((components, pixels // LANES, 2 * band_rows, LANES), jnp.float32),
            pltpu.VMEM((components, pixels, pixels), jnp.float32),
            pltpu.VMEM((modes, pixels, 2 * pixels), jnp.float32),
            pltpu.VMEM((modes, pixels, 2 * pixels), jnp.float32),
            pltpu.VMEM((pixels, pixels), jnp.float32),
        ],
        cost_estimate=pl.CostEstimate(flops=products, bytes_accessed=12 * 2**20, transcendentals=0),
        compiler_params=pltpu.CompilerParams(vmem_limit_bytes=48 * 1024 * 1024),
    )(place, tiles, halo, probe, wave, measured, matrices)


def scatter_kernel(row_ref, column_ref, patch_ref, own_ref, spill_ref, canvas):
    count, pixels = patch_ref.shape[0], patch_ref.shape[1]
    band_rows = own_ref.shape[1]
    canvas[...] = jnp.zeros_like(canvas)

    def body(index, carry):
        row = row_ref[index]
        column = column_ref[index]
        first = column // LANES
        shift = column % LANES
        left = pltpu.roll(patch_ref[index, :, :LANES], shift, 1)
        right = pltpu.roll(patch_ref[index, :, LANES:], shift, 1)
        lane = lax.broadcasted_iota(jnp.int32, left.shape, 1)
        late = lane >= shift
        zero = jnp.zeros_like(left)
        rows = pl.ds(row, pixels)
        canvas[first, rows, :] += jnp.where(late, left, zero)
        canvas[first + 1, rows, :] += jnp.where(late, right, left)
        canvas[first + 2, rows, :] += jnp.where(late, zero, right)
        return carry

    lax.fori_loop(0, count, body, 0)
    tiles = own_ref.shape[0]
    own_ref[...] = canvas[:tiles, :band_rows, :]
    spill_ref[...] = canvas[:tiles, band_rows:, :]


def scatter(rows, columns, patches, band_rows):
    shape = jax.ShapeDtypeStruct((TGX, band_rows, LANES), jnp.float32)
    return pl.pallas_call(
        scatter_kernel,
        out_shape=(shape, shape),
        in_specs=[scalar_spec(), scalar_spec(), full_spec()],
        out_specs=(full_spec(), full_spec()),
        scratch_shapes=[pltpu.VMEM((TGX + 1, 2 * band_rows, LANES), jnp.float32)],
        compiler_params=pltpu.CompilerParams(vmem_limit_bytes=32 * 1024 * 1024),
    )(rows, columns, patches)


def dense_update(object_tiles, gradients, rows, columns, band_rows):
    _, slices, _, side, _ = object_tiles.shape
    components, pixels = gradients[0].shape[0], gradients[0].shape[1]
    band_tiles = band_rows // side
    canvas = jnp.zeros((components, 2 * band_rows, TGX * side), jnp.float32)
    zero = jnp.int32(0)
    for slot, gradient in enumerate(gradients):
        corner = (zero, rows[slot], columns[slot])
        former = lax.dynamic_slice(canvas, corner, gradient.shape)
        canvas = lax.dynamic_update_slice(canvas, former + gradient, corner)
    shaped = canvas.reshape(components, 2, band_tiles, side, TGX, side).transpose(1, 2, 4, 0, 3, 5)
    shaped = shaped.reshape(2, -1, side)
    combined = lax.psum(shaped[0] + shifted(shaped[1], "region", 1), "pos")
    return object_tiles - step_size * combined.reshape(object_tiles.shape)


def per_device(object_tiles, probe, fresnel_phase, patterns, row_offsets, col_offsets, counts):
    slots = patterns.shape[2]
    pixels = patterns.shape[-1]
    held, slices, _, side, _ = object_tiles.shape
    components = 2 * slices
    band_tiles = held // TGX
    band_rows = band_tiles * side
    groups = lax.axis_size("pos")
    me = lax.axis_index("pos")
    tiles = object_tiles.reshape(held, components, side, side)
    measured = patterns.reshape(slots, pixels, pixels)
    rows = row_offsets.reshape(slots) - lax.axis_index("region") * band_rows
    columns = col_offsets.reshape(slots)
    live = (jnp.arange(slots, dtype=jnp.int32) < counts.reshape(())).astype(jnp.int32)

    wanted = shifted(columns, "region", 1)
    windows = column_windows(wanted, tiles, pixels)
    halos = [shifted(windows[slot], "region", -1) for slot in range(slots)]

    matrices = make_matrices(pixels)
    wave = jnp.stack([jnp.cos(fresnel_phase), jnp.sin(fresnel_phase)])
    places = jnp.stack([rows, columns, live], axis=1)

    gradients = [
        position_gradient(places[slot], tiles, halos[slot], probe, wave, measured[slot], matrices)
        for slot in range(slots)
    ]
    if groups != components:
        return dense_update(object_tiles, gradients, rows, columns, band_rows)

    corner = jnp.stack([rows, columns])
    corners = [corner] + [rotated(corner, "pos", by) for by in range(1, groups)]
    parts = []
    for gradient in gradients:
        for by in range(groups):
            piece = lax.dynamic_index_in_dim(gradient, lax.rem(me + by, groups), 0, keepdims=False)
            parts.append(piece if by == 0 else rotated(piece, "pos", by))
    all_rows = jnp.stack([corners[by][0, slot] for slot in range(slots) for by in range(groups)])
    all_columns = jnp.stack([corners[by][1, slot] for slot in range(slots) for by in range(groups)])
    own, spill = scatter(all_rows, all_columns, jnp.stack(parts), band_rows)
    arrived = shifted(spill, "region", 1)
    total = (own + arrived).reshape(TGX, band_tiles, side, side).transpose(1, 0, 2, 3)
    total = total.reshape(held, side, side)
    mine = lax.dynamic_index_in_dim(tiles, me, 1, keepdims=False) - step_size * total

    rightward, leftward = [mine], [mine]
    for _ in range(groups - 1):
        rightward.append(shifted(rightward[-1], "pos", 1))
        leftward.append(shifted(leftward[-1], "pos", -1))
    found = [mine] + [leftward[by] + rightward[groups - by] for by in range(1, groups)]
    result = jnp.zeros_like(tiles)
    for by in range(groups):
        result = lax.dynamic_update_slice_in_dim(
            result, found[by][:, None], lax.rem(me + by, groups), 1
        )
    return result.reshape(object_tiles.shape)


def solution(mesh):
    in_specs = (
        P("region", None, None, None, None),
        P(),
        P(),
        P("region", "pos", None, None, None),
        P("region", "pos", None),
        P("region", "pos", None),
        P("region", "pos"),
    )
    out_specs = P("region", None, None, None, None)
    return jax.shard_map(
        per_device, mesh=mesh, in_specs=in_specs, out_specs=out_specs, check_vma=False
    )
```

```python
import functools
import math

import jax
import jax.numpy as jnp
from jax import lax
from jax.experimental import pallas as pl
from jax.experimental.pallas import tpu as pltpu
from jax.sharding import PartitionSpec as P

TGX = 8
LANES = 128
MARK = 8
CODE = 4096
CHUNKS = 4
MESH = pl.DeviceIdType.MESH

step_size = 0.05


def shifted(shard, axis, by):
    count = lax.axis_size(axis)
    pairs = [(i, i + by) for i in range(count) if 0 <= i + by < count]
    return lax.ppermute(shard, axis, pairs)


def rotated(shard, axis, by):
    count = lax.axis_size(axis)
    return lax.ppermute(shard, axis, [(i, (i + by) % count) for i in range(count)])


def make_tables(length):
    counter = jnp.arange(length, dtype=jnp.int32)
    product = counter[:, None] * counter[None, :] % length
    angles = product.astype(jnp.float32) * jnp.float32(2.0 * math.pi / length)
    factor = jnp.float32(1.0 / math.sqrt(length))
    return (
        (jnp.cos(angles) * factor).astype(jnp.bfloat16),
        (jnp.sin(angles) * factor).astype(jnp.bfloat16),
    )


def make_matrices(length):
    cos_table, sin_table = make_tables(length)
    plus = jnp.concatenate(
        [
            jnp.concatenate([cos_table, -sin_table], axis=1),
            jnp.concatenate([sin_table, cos_table], axis=1),
        ],
        axis=0,
    )
    minus = jnp.concatenate(
        [
            jnp.concatenate([cos_table, sin_table], axis=1),
            jnp.concatenate([-sin_table, cos_table], axis=1),
        ],
        axis=0,
    )
    return jnp.stack([plus, minus])


def full_spec():
    return pl.BlockSpec(memory_space=pltpu.VMEM)


def scalar_spec():
    return pl.BlockSpec(memory_space=pltpu.SMEM)


def store_columns(tiles_ref, base, component, column, write):
    first = column // LANES
    shift = column % LANES
    back = (LANES - shift) % LANES
    third = jnp.minimum(first + 2, TGX - 1)
    left = pltpu.roll(tiles_ref[base + first, component], back, 1)
    middle = pltpu.roll(tiles_ref[base + first + 1, component], back, 1)
    right = pltpu.roll(tiles_ref[base + third, component], back, 1)
    lane = lax.broadcasted_iota(jnp.int32, left.shape, 1)
    keep = lane < LANES - shift
    write(0, jnp.where(keep, left, middle))
    write(1, jnp.where(keep, middle, right))


def window_kernel(column_ref, tiles_ref, out_ref):
    slots = out_ref.shape[0]
    components = tiles_ref.shape[1]
    side = tiles_ref.shape[2]
    rows = tiles_ref.shape[0] // TGX
    for slot in range(slots):
        column = column_ref[slot]

        def body(component, carry):
            for row in range(rows):

                def write(half, value):
                    out_ref[
                        slot, component, row * side : (row + 1) * side, half * LANES : (half + 1) * LANES
                    ] = value

                store_columns(tiles_ref, row * TGX, component, column, write)
            return carry

        lax.fori_loop(0, components, body, 0)


def column_windows(columns, tiles, pixels):
    band = tiles.shape[0] // TGX * tiles.shape[2]
    return pl.pallas_call(
        window_kernel,
        out_shape=jax.ShapeDtypeStruct((columns.shape[0], tiles.shape[1], band, pixels), jnp.float32),
        in_specs=[scalar_spec(), full_spec()],
        out_specs=full_spec(),
        compiler_params=pltpu.CompilerParams(vmem_limit_bytes=32 * 1024 * 1024),
    )(columns, tiles)


def position_kernel(
    place_ref,
    tiles_ref,
    halo_ref,
    probe_ref,
    wave_ref,
    measured_ref,
    matrix_ref,
    out_ref,
    canvas,
    patch,
    field,
    far,
    intensity,
):
    row = place_ref[0]
    column = place_ref[1]
    live = place_ref[2]
    components, pixels = patch.shape[0], patch.shape[1]
    modes = probe_ref.shape[0]
    side = tiles_ref.shape[2]
    band_tiles = tiles_ref.shape[0] // TGX
    band_rows = band_tiles * side
    plus, minus = 0, 1

    def fill(component, carry):
        for tile_row in range(band_tiles):

            def write(half, value):
                canvas[component, half, tile_row * side : (tile_row + 1) * side, :] = value

            store_columns(tiles_ref, tile_row * TGX, component, column, write)
        for half in range(pixels // LANES):
            lanes = slice(half * LANES, (half + 1) * LANES)
            canvas[component, half, band_rows:, :] = halo_ref[component, :, lanes]
            patch[component, :, lanes] = canvas[component, half, pl.ds(row, pixels), :]
        return carry

    lax.fori_loop(0, components, fill, 0)

    def transform(real, imag, left, right):
        stacked = jnp.concatenate([real, imag], axis=0).astype(jnp.bfloat16)
        upper = jnp.dot(matrix_ref[left], stacked, preferred_element_type=jnp.float32)
        upper = upper.astype(jnp.bfloat16)
        upper = jnp.concatenate([upper[:pixels], upper[pixels:]], axis=1)
        return jnp.dot(upper, matrix_ref[right], preferred_element_type=jnp.float32)

    def forward_transform(real, imag):
        return transform(real, imag, minus, plus)

    def inverse_transform(real, imag):
        return transform(real, imag, plus, minus)

    intensity[...] = jnp.zeros_like(intensity)

    def forward(mode, carry):
        field_re, field_im = probe_ref[mode, 0], probe_ref[mode, 1]
        spec = forward_transform(
            field_re * patch[0] - field_im * patch[1],
            field_re * patch[1] + field_im * patch[0],
        )
        spec_re, spec_im = spec[:, :pixels], spec[:, pixels:]
        moved = inverse_transform(
            wave_ref[0] * spec_re - wave_ref[1] * spec_im,
            wave_ref[0] * spec_im + wave_ref[1] * spec_re,
        )
        field[mode] = moved
        field_re, field_im = moved[:, :pixels], moved[:, pixels:]
        psi = forward_transform(
            field_re * patch[2] - field_im * patch[3],
            field_re * patch[3] + field_im * patch[2],
        )
        far[mode] = psi
        psi_re, psi_im = psi[:, :pixels], psi[:, pixels:]
        intensity[...] += psi_re * psi_re + psi_im * psi_im
        return carry

    lax.fori_loop(0, modes, forward, 0, unroll=4)

    intensity[...] -= measured_ref[...]
    out_ref[...] = jnp.zeros_like(out_ref)

    def backward(mode, carry):
        misfit = intensity[...]
        psi = far[mode]
        back = inverse_transform(misfit * psi[:, :pixels], misfit * psi[:, pixels:])
        back_re, back_im = back[:, :pixels], back[:, pixels:]
        field_re, field_im = field[mode, :, :pixels], field[mode, :, pixels:]
        out_ref[2, :pixels] += field_re * back_re + field_im * back_im
        out_ref[3, :pixels] += field_re * back_im - field_im * back_re
        spec = forward_transform(
            patch[2] * back_re + patch[3] * back_im,
            patch[2] * back_im - patch[3] * back_re,
        )
        spec_re, spec_im = spec[:, :pixels], spec[:, pixels:]
        back = inverse_transform(
            wave_ref[0] * spec_re + wave_ref[1] * spec_im,
            wave_ref[0] * spec_im - wave_ref[1] * spec_re,
        )
        back_re, back_im = back[:, :pixels], back[:, pixels:]
        field_re, field_im = probe_ref[mode, 0], probe_ref[mode, 1]
        out_ref[0, :pixels] += field_re * back_re + field_im * back_im
        out_ref[1, :pixels] += field_re * back_im - field_im * back_re
        return carry

    lax.fori_loop(0, modes, backward, 0, unroll=4)

    @pl.when(live == 0)
    def _():
        out_ref[...] = jnp.zeros_like(out_ref)

    code = (row * CODE + column).astype(jnp.float32)
    out_ref[:, pixels:, :] = jnp.full((components, MARK, pixels), code)


def position_gradient(place, tiles, halo, probe, wave, measured, matrices):
    components = tiles.shape[1]
    modes, _, pixels, _ = probe.shape
    band_rows = tiles.shape[0] // TGX * tiles.shape[2]
    products = 6 * modes * 2 * 2 * (2 * pixels) ** 2 * pixels
    return pl.pallas_call(
        position_kernel,
        out_shape=jax.ShapeDtypeStruct((components, pixels + MARK, pixels), jnp.float32),
        in_specs=[scalar_spec()] + [full_spec()] * 6,
        out_specs=full_spec(),
        scratch_shapes=[
            pltpu.VMEM((components, pixels // LANES, 2 * band_rows, LANES), jnp.float32),
            pltpu.VMEM((components, pixels, pixels), jnp.float32),
            pltpu.VMEM((modes, pixels, 2 * pixels), jnp.float32),
            pltpu.VMEM((modes, pixels, 2 * pixels), jnp.float32),
            pltpu.VMEM((pixels, pixels), jnp.float32),
        ],
        cost_estimate=pl.CostEstimate(flops=products, bytes_accessed=12 * 2**20, transcendentals=0),
        compiler_params=pltpu.CompilerParams(vmem_limit_bytes=48 * 1024 * 1024),
    )(place, tiles, halo, probe, wave, measured, matrices)


def scatter_kernel(*refs):
    *patch_refs, own_ref, spill_ref, canvas = refs
    pixels = patch_refs[0].shape[1]
    band_rows = own_ref.shape[1]
    canvas[...] = jnp.zeros_like(canvas)
    for patch_ref in patch_refs:
        code = jnp.max(patch_ref[pixels:, :LANES]).astype(jnp.int32)
        row = lax.div(code, CODE)
        column = lax.rem(code, CODE)
        first = lax.div(column, LANES)
        shift = lax.rem(column, LANES)
        left = pltpu.roll(patch_ref[:pixels, :LANES], shift, 1)
        right = pltpu.roll(patch_ref[:pixels, LANES:], shift, 1)
        lane = lax.broadcasted_iota(jnp.int32, left.shape, 1)
        late = lane >= shift
        zero = jnp.zeros_like(left)
        rows = pl.ds(row, pixels)
        canvas[first, rows, :] += jnp.where(late, left, zero)
        canvas[first + 1, rows, :] += jnp.where(late, right, left)
        canvas[first + 2, rows, :] += jnp.where(late, zero, right)
    tiles = own_ref.shape[0]
    own_ref[...] = canvas[:tiles, :band_rows, :]
    spill_ref[...] = canvas[:tiles, band_rows:, :]


def scatter(patches, band_rows):
    shape = jax.ShapeDtypeStruct((TGX, band_rows, LANES), jnp.float32)
    return pl.pallas_call(
        scatter_kernel,
        out_shape=(shape, shape),
        in_specs=[full_spec()] * len(patches),
        out_specs=(full_spec(), full_spec()),
        scratch_shapes=[pltpu.VMEM((TGX + 1, 2 * band_rows, LANES), jnp.float32)],
        compiler_params=pltpu.CompilerParams(vmem_limit_bytes=32 * 1024 * 1024),
    )(*patches)


def finish_kernel(
    regions,
    groups,
    tiles_ref,
    own_ref,
    spill_ref,
    out_ref,
    arrived,
    spill_send,
    spill_recv,
    right_send,
    right_recv,
    left_send,
    left_recv,
):
    band = lax.axis_index("region")
    me = lax.axis_index("pos")
    band_tiles, across, side, _ = tiles_ref.shape
    width = across // CHUNKS
    above, below = band > 0, band < regions - 1
    has_left, has_right = me > 0, me < groups - 1
    partners = (
        (above, {"region": band - 1}),
        (below, {"region": band + 1}),
        (has_left, {"pos": me - 1}),
        (has_right, {"pos": me + 1}),
    )

    barrier = pltpu.get_barrier_semaphore()
    for exists, where in partners:

        @pl.when(exists)
        def _():
            pl.semaphore_signal(barrier, inc=1, device_id=where, device_id_type=MESH)

    pl.semaphore_wait(barrier, sum(exists.astype(jnp.int32) for exists, _ in partners))

    def columns(chunk):
        return slice(chunk * width, (chunk + 1) * width)

    def spill_copy(chunk):
        return pltpu.make_async_remote_copy(
            src_ref=spill_ref.at[columns(chunk)],
            dst_ref=arrived.at[columns(chunk)],
            send_sem=spill_send.at[chunk],
            recv_sem=spill_recv.at[chunk],
            device_id={"region": band + 1},
            device_id_type=MESH,
        )

    def rightward(owner, step, chunk):
        part = out_ref.at[:, columns(chunk), owner]
        return pltpu.make_async_remote_copy(
            src_ref=part,
            dst_ref=part,
            send_sem=right_send.at[step, chunk],
            recv_sem=right_recv.at[step, chunk],
            device_id={"pos": me + 1},
            device_id_type=MESH,
        )

    def leftward(owner, step, chunk):
        part = out_ref.at[:, columns(chunk), owner]
        return pltpu.make_async_remote_copy(
            src_ref=part,
            dst_ref=part,
            send_sem=left_send.at[step, chunk],
            recv_sem=left_recv.at[step, chunk],
            device_id={"pos": me - 1},
            device_id_type=MESH,
        )

    @pl.when(below)
    def _():
        for chunk in range(CHUNKS):
            spill_copy(chunk).start()

    @pl.when(band == 0)
    def _():
        arrived[...] = jnp.zeros_like(arrived)

    for chunk in range(CHUNKS):

        @pl.when(above)
        def _():
            spill_copy(chunk).wait_recv()

        for tile in range(chunk * width, (chunk + 1) * width):
            for row in range(band_tiles):
                lines = slice(row * side, (row + 1) * side)
                total = own_ref[tile, lines, :] + arrived[tile, lines, :]
                out_ref[row, tile, me] = tiles_ref[row, tile] - step_size * total

        @pl.when(has_right)
        def _():
            rightward(me, 0, chunk).start()

        @pl.when(has_left)
        def _():
            leftward(me, 0, chunk).start()

    for step in range(1, groups):
        for chunk in range(CHUNKS):

            @pl.when(me >= step)
            def _():
                rightward(me - step, step - 1, chunk).wait_recv()

            if step < groups - 1:

                @pl.when((me >= step) & has_right)
                def _():
                    rightward(me - step, step, chunk).start()

            @pl.when(me + step < groups)
            def _():
                leftward(me + step, step - 1, chunk).wait_recv()

            if step < groups - 1:

                @pl.when((me + step < groups) & has_left)
                def _():
                    leftward(me + step, step, chunk).start()

    for chunk in range(CHUNKS):

        @pl.when(below)
        def _():
            spill_copy(chunk).wait_send()

        for step in range(groups - 1):

            @pl.when((me >= step) & has_right)
            def _():
                rightward(me - step, step, chunk).wait_send()

            @pl.when((me + step < groups) & has_left)
            def _():
                leftward(me + step, step, chunk).wait_send()


def finish(tiles, own, spill, groups, regions):
    band_tiles, across, side, _ = tiles.shape
    sems = pltpu.SemaphoreType.DMA((groups - 1, CHUNKS))
    return pl.pallas_call(
        functools.partial(finish_kernel, regions, groups),
        out_shape=jax.ShapeDtypeStruct((band_tiles, across, groups, side, side), jnp.float32),
        in_specs=[full_spec()] * 3,
        out_specs=full_spec(),
        scratch_shapes=[
            pltpu.VMEM(own.shape, jnp.float32),
            pltpu.SemaphoreType.DMA((CHUNKS,)),
            pltpu.SemaphoreType.DMA((CHUNKS,)),
            sems,
            sems,
            sems,
            sems,
        ],
        compiler_params=pltpu.CompilerParams(
            collective_id=0, has_side_effects=True, vmem_limit_bytes=32 * 1024 * 1024
        ),
    )(tiles, own, spill)


def dense_update(object_tiles, gradients, rows, columns, band_rows):
    _, slices, _, side, _ = object_tiles.shape
    components, pixels = gradients[0].shape[0], gradients[0].shape[1]
    band_tiles = band_rows // side
    canvas = jnp.zeros((components, 2 * band_rows, TGX * side), jnp.float32)
    zero = jnp.int32(0)
    for slot, gradient in enumerate(gradients):
        corner = (zero, rows[slot], columns[slot])
        former = lax.dynamic_slice(canvas, corner, gradient.shape)
        canvas = lax.dynamic_update_slice(canvas, former + gradient, corner)
    shaped = canvas.reshape(components, 2, band_tiles, side, TGX, side).transpose(1, 2, 4, 0, 3, 5)
    shaped = shaped.reshape(2, -1, side)
    combined = lax.psum(shaped[0] + shifted(shaped[1], "region", 1), "pos")
    return object_tiles - step_size * combined.reshape(object_tiles.shape)


def per_device(object_tiles, probe, fresnel_phase, patterns, row_offsets, col_offsets, counts):
    slots = patterns.shape[2]
    pixels = patterns.shape[-1]
    held, slices, _, side, _ = object_tiles.shape
    components = 2 * slices
    band_tiles = held // TGX
    band_rows = band_tiles * side
    groups = lax.axis_size("pos")
    me = lax.axis_index("pos")
    tiles = object_tiles.reshape(held, components, side, side)
    measured = patterns.reshape(slots, pixels, pixels)
    rows = row_offsets.reshape(slots) - lax.axis_index("region") * band_rows
    columns = col_offsets.reshape(slots)
    live = (jnp.arange(slots, dtype=jnp.int32) < counts.reshape(())).astype(jnp.int32)

    wanted = shifted(columns, "region", 1)
    windows = column_windows(wanted, tiles, pixels)
    halos = [shifted(windows[slot], "region", -1) for slot in range(slots)]

    matrices = make_matrices(pixels)
    wave = jnp.stack([jnp.cos(fresnel_phase), jnp.sin(fresnel_phase)])
    places = jnp.stack([rows, columns, live], axis=1)

    gradients = [
        position_gradient(places[slot], tiles, halos[slot], probe, wave, measured[slot], matrices)
        for slot in range(slots)
    ]
    if groups != components:
        gradients = [gradient[:, :pixels] for gradient in gradients]
        return dense_update(object_tiles, gradients, rows, columns, band_rows)

    parts = []
    for gradient in gradients:
        for by in range(groups):
            piece = lax.dynamic_index_in_dim(gradient, lax.rem(me + by, groups), 0, keepdims=False)
            parts.append(piece if by == 0 else rotated(piece, "pos", by))
    own, spill = scatter(parts, band_rows)
    mine = lax.dynamic_index_in_dim(tiles, me, 1, keepdims=False)
    mine = mine.reshape(band_tiles, TGX, side, side)
    result = finish(mine, own, spill, groups, lax.axis_size("region"))
    return result.reshape(object_tiles.shape)


def solution(mesh):
    in_specs = (
        P("region", None, None, None, None),
        P(),
        P(),
        P("region", "pos", None, None, None),
        P("region", "pos", None),
        P("region", "pos", None),
        P("region", "pos"),
    )
    out_specs = P("region", None, None, None, None)
    return jax.shard_map(
        per_device, mesh=mesh, in_specs=in_specs, out_specs=out_specs, check_vma=False
    )
```

```python
import functools
import math

import jax
import jax.numpy as jnp
from jax import lax
from jax.experimental import pallas as pl
from jax.experimental.pallas import tpu as pltpu
from jax.sharding import PartitionSpec as P

TGX = 8
LANES = 128
MARK = 8
CODE = 4096
CHUNKS = 4
MESH = pl.DeviceIdType.MESH

step_size = 0.05


def shifted(shard, axis, by):
    count = lax.axis_size(axis)
    pairs = [(i, i + by) for i in range(count) if 0 <= i + by < count]
    return lax.ppermute(shard, axis, pairs)


def rotated(shard, axis, by):
    count = lax.axis_size(axis)
    return lax.ppermute(shard, axis, [(i, (i + by) % count) for i in range(count)])


def make_tables(length):
    counter = jnp.arange(length, dtype=jnp.int32)
    product = counter[:, None] * counter[None, :] % length
    angles = product.astype(jnp.float32) * jnp.float32(2.0 * math.pi / length)
    factor = jnp.float32(1.0 / math.sqrt(length))
    return (
        (jnp.cos(angles) * factor).astype(jnp.bfloat16),
        (jnp.sin(angles) * factor).astype(jnp.bfloat16),
    )


def make_matrices(length):
    cos_table, sin_table = make_tables(length)
    plus = jnp.concatenate(
        [
            jnp.concatenate([cos_table, -sin_table], axis=1),
            jnp.concatenate([sin_table, cos_table], axis=1),
        ],
        axis=0,
    )
    minus = jnp.concatenate(
        [
            jnp.concatenate([cos_table, sin_table], axis=1),
            jnp.concatenate([-sin_table, cos_table], axis=1),
        ],
        axis=0,
    )
    return jnp.stack([plus, minus])


def full_spec():
    return pl.BlockSpec(memory_space=pltpu.VMEM)


def scalar_spec():
    return pl.BlockSpec(memory_space=pltpu.SMEM)


def store_columns(tiles_ref, base, component, column, write):
    first = column // LANES
    shift = column % LANES
    back = (LANES - shift) % LANES
    third = jnp.minimum(first + 2, TGX - 1)
    left = pltpu.roll(tiles_ref[base + first, component], back, 1)
    middle = pltpu.roll(tiles_ref[base + first + 1, component], back, 1)
    right = pltpu.roll(tiles_ref[base + third, component], back, 1)
    lane = lax.broadcasted_iota(jnp.int32, left.shape, 1)
    keep = lane < LANES - shift
    write(0, jnp.where(keep, left, middle))
    write(1, jnp.where(keep, middle, right))


def window_kernel(column_ref, tiles_ref, out_ref):
    slots = out_ref.shape[0]
    components = tiles_ref.shape[1]
    side = tiles_ref.shape[2]
    rows = tiles_ref.shape[0] // TGX
    for slot in range(slots):
        column = column_ref[slot]

        def body(component, carry):
            for row in range(rows):

                def write(half, value):
                    out_ref[
                        slot, component, row * side : (row + 1) * side, half * LANES : (half + 1) * LANES
                    ] = value

                store_columns(tiles_ref, row * TGX, component, column, write)
            return carry

        lax.fori_loop(0, components, body, 0)


def column_windows(columns, tiles, pixels):
    band = tiles.shape[0] // TGX * tiles.shape[2]
    return pl.pallas_call(
        window_kernel,
        out_shape=jax.ShapeDtypeStruct((columns.shape[0], tiles.shape[1], band, pixels), jnp.float32),
        in_specs=[scalar_spec(), full_spec()],
        out_specs=full_spec(),
        compiler_params=pltpu.CompilerParams(vmem_limit_bytes=32 * 1024 * 1024),
    )(columns, tiles)


def position_kernel(
    place_ref,
    tiles_ref,
    halo_ref,
    probe_ref,
    wave_ref,
    measured_ref,
    matrix_ref,
    out_ref,
    canvas,
    patch,
    field,
    far,
    intensity,
    stacked,
    middle,
):
    row = place_ref[0]
    column = place_ref[1]
    live = place_ref[2]
    components, pixels = patch.shape[0], patch.shape[1]
    modes = probe_ref.shape[0]
    side = tiles_ref.shape[2]
    band_tiles = tiles_ref.shape[0] // TGX
    band_rows = band_tiles * side
    plus, minus = 0, 1

    def fill(component, carry):
        for tile_row in range(band_tiles):

            def write(half, value):
                canvas[component, half, tile_row * side : (tile_row + 1) * side, :] = value

            store_columns(tiles_ref, tile_row * TGX, component, column, write)
        for half in range(pixels // LANES):
            lanes = slice(half * LANES, (half + 1) * LANES)
            canvas[component, half, band_rows:, :] = halo_ref[component, :, lanes]
            patch[component, :, lanes] = canvas[component, half, pl.ds(row, pixels), :]
        return carry

    lax.fori_loop(0, components, fill, 0)

    def transform(left, right):
        upper = jnp.dot(matrix_ref[left], stacked[...], preferred_element_type=jnp.float32)
        for mode in range(modes):
            lines = slice(mode * pixels, (mode + 1) * pixels)
            middle[lines, :pixels] = upper[:pixels, lines].astype(jnp.bfloat16)
            middle[lines, pixels:] = upper[pixels:, lines].astype(jnp.bfloat16)
        return jnp.dot(middle[...], matrix_ref[right], preferred_element_type=jnp.float32)

    def forward_transform():
        return transform(minus, plus)

    def inverse_transform():
        return transform(plus, minus)

    def put(mode, real, imag):
        lanes = slice(mode * pixels, (mode + 1) * pixels)
        stacked[:pixels, lanes] = real.astype(jnp.bfloat16)
        stacked[pixels:, lanes] = imag.astype(jnp.bfloat16)

    def pick(value, mode):
        lines = value[mode * pixels : (mode + 1) * pixels]
        return lines[:, :pixels], lines[:, pixels:]

    for mode in range(modes):
        u_re, u_im = probe_ref[mode, 0], probe_ref[mode, 1]
        put(mode, u_re * patch[0] - u_im * patch[1], u_re * patch[1] + u_im * patch[0])
    spec = forward_transform()
    for mode in range(modes):
        re, im = pick(spec, mode)
        put(mode, wave_ref[0] * re - wave_ref[1] * im, wave_ref[0] * im + wave_ref[1] * re)
    moved = inverse_transform()
    for mode in range(modes):
        u_re, u_im = pick(moved, mode)
        field[mode, :, :pixels] = u_re
        field[mode, :, pixels:] = u_im
        put(mode, u_re * patch[2] - u_im * patch[3], u_re * patch[3] + u_im * patch[2])
    psi = forward_transform()
    total = -measured_ref[...]
    for mode in range(modes):
        re, im = pick(psi, mode)
        far[mode, :, :pixels] = re
        far[mode, :, pixels:] = im
        total += re * re + im * im
    intensity[...] = total
    for mode in range(modes):
        put(mode, intensity[...] * far[mode, :, :pixels], intensity[...] * far[mode, :, pixels:])
    back = inverse_transform()
    grad_re, grad_im = 0.0, 0.0
    for mode in range(modes):
        b_re, b_im = pick(back, mode)
        u_re, u_im = field[mode, :, :pixels], field[mode, :, pixels:]
        grad_re += u_re * b_re + u_im * b_im
        grad_im += u_re * b_im - u_im * b_re
        put(mode, patch[2] * b_re + patch[3] * b_im, patch[2] * b_im - patch[3] * b_re)
    out_ref[2, :pixels] = grad_re
    out_ref[3, :pixels] = grad_im
    spec = forward_transform()
    for mode in range(modes):
        re, im = pick(spec, mode)
        put(mode, wave_ref[0] * re + wave_ref[1] * im, wave_ref[0] * im - wave_ref[1] * re)
    back = inverse_transform()
    grad_re, grad_im = 0.0, 0.0
    for mode in range(modes):
        b_re, b_im = pick(back, mode)
        u_re, u_im = probe_ref[mode, 0], probe_ref[mode, 1]
        grad_re += u_re * b_re + u_im * b_im
        grad_im += u_re * b_im - u_im * b_re
    out_ref[0, :pixels] = grad_re
    out_ref[1, :pixels] = grad_im

    @pl.when(live == 0)
    def _():
        out_ref[...] = jnp.zeros_like(out_ref)

    code = (row * CODE + column).astype(jnp.float32)
    out_ref[:, pixels:, :] = jnp.full((components, MARK, pixels), code)


def position_gradient(place, tiles, halo, probe, wave, measured, matrices):
    components = tiles.shape[1]
    modes, _, pixels, _ = probe.shape
    band_rows = tiles.shape[0] // TGX * tiles.shape[2]
    products = 6 * modes * 2 * 2 * (2 * pixels) ** 2 * pixels
    return pl.pallas_call(
        position_kernel,
        out_shape=jax.ShapeDtypeStruct((components, pixels + MARK, pixels), jnp.float32),
        in_specs=[scalar_spec()] + [full_spec()] * 6,
        out_specs=full_spec(),
        scratch_shapes=[
            pltpu.VMEM((components, pixels // LANES, 2 * band_rows, LANES), jnp.float32),
            pltpu.VMEM((components, pixels, pixels), jnp.float32),
            pltpu.VMEM((modes, pixels, 2 * pixels), jnp.float32),
            pltpu.VMEM((modes, pixels, 2 * pixels), jnp.float32),
            pltpu.VMEM((pixels, pixels), jnp.float32),
            pltpu.VMEM((2 * pixels, modes * pixels), jnp.bfloat16),
            pltpu.VMEM((modes * pixels, 2 * pixels), jnp.bfloat16),
        ],
        cost_estimate=pl.CostEstimate(flops=products, bytes_accessed=12 * 2**20, transcendentals=0),
        compiler_params=pltpu.CompilerParams(vmem_limit_bytes=48 * 1024 * 1024),
    )(place, tiles, halo, probe, wave, measured, matrices)


def scatter_kernel(*refs):
    *patch_refs, own_ref, spill_ref, canvas = refs
    pixels = patch_refs[0].shape[1]
    band_rows = own_ref.shape[1]
    canvas[...] = jnp.zeros_like(canvas)
    for patch_ref in patch_refs:
        code = jnp.max(patch_ref[pixels:, :LANES]).astype(jnp.int32)
        row = lax.div(code, CODE)
        column = lax.rem(code, CODE)
        first = lax.div(column, LANES)
        shift = lax.rem(column, LANES)
        left = pltpu.roll(patch_ref[:pixels, :LANES], shift, 1)
        right = pltpu.roll(patch_ref[:pixels, LANES:], shift, 1)
        lane = lax.broadcasted_iota(jnp.int32, left.shape, 1)
        late = lane >= shift
        zero = jnp.zeros_like(left)
        rows = pl.ds(row, pixels)
        canvas[first, rows, :] += jnp.where(late, left, zero)
        canvas[first + 1, rows, :] += jnp.where(late, right, left)
        canvas[first + 2, rows, :] += jnp.where(late, zero, right)
    tiles = own_ref.shape[0]
    own_ref[...] = canvas[:tiles, :band_rows, :]
    spill_ref[...] = canvas[:tiles, band_rows:, :]


def scatter(patches, band_rows):
    shape = jax.ShapeDtypeStruct((TGX, band_rows, LANES), jnp.float32)
    return pl.pallas_call(
        scatter_kernel,
        out_shape=(shape, shape),
        in_specs=[full_spec()] * len(patches),
        out_specs=(full_spec(), full_spec()),
        scratch_shapes=[pltpu.VMEM((TGX + 1, 2 * band_rows, LANES), jnp.float32)],
        compiler_params=pltpu.CompilerParams(vmem_limit_bytes=32 * 1024 * 1024),
    )(*patches)


def finish_kernel(
    regions,
    groups,
    tiles_ref,
    own_ref,
    spill_ref,
    out_ref,
    arrived,
    spill_send,
    spill_recv,
    right_send,
    right_recv,
    left_send,
    left_recv,
):
    band = lax.axis_index("region")
    me = lax.axis_index("pos")
    band_tiles, across, side, _ = tiles_ref.shape
    width = across // CHUNKS
    above, below = band > 0, band < regions - 1
    has_left, has_right = me > 0, me < groups - 1
    partners = (
        (above, {"region": band - 1}),
        (below, {"region": band + 1}),
        (has_left, {"pos": me - 1}),
        (has_right, {"pos": me + 1}),
    )

    barrier = pltpu.get_barrier_semaphore()
    for exists, where in partners:

        @pl.when(exists)
        def _():
            pl.semaphore_signal(barrier, inc=1, device_id=where, device_id_type=MESH)

    pl.semaphore_wait(barrier, sum(exists.astype(jnp.int32) for exists, _ in partners))

    def columns(chunk):
        return slice(chunk * width, (chunk + 1) * width)

    def spill_copy(chunk):
        return pltpu.make_async_remote_copy(
            src_ref=spill_ref.at[columns(chunk)],
            dst_ref=arrived.at[columns(chunk)],
            send_sem=spill_send.at[chunk],
            recv_sem=spill_recv.at[chunk],
            device_id={"region": band + 1},
            device_id_type=MESH,
        )

    def rightward(owner, step, chunk):
        part = out_ref.at[:, columns(chunk), owner]
        return pltpu.make_async_remote_copy(
            src_ref=part,
            dst_ref=part,
            send_sem=right_send.at[step, chunk],
            recv_sem=right_recv.at[step, chunk],
            device_id={"pos": me + 1},
            device_id_type=MESH,
        )

    def leftward(owner, step, chunk):
        part = out_ref.at[:, columns(chunk), owner]
        return pltpu.make_async_remote_copy(
            src_ref=part,
            dst_ref=part,
            send_sem=left_send.at[step, chunk],
            recv_sem=left_recv.at[step, chunk],
            device_id={"pos": me - 1},
            device_id_type=MESH,
        )

    @pl.when(below)
    def _():
        for chunk in range(CHUNKS):
            spill_copy(chunk).start()

    @pl.when(band == 0)
    def _():
        arrived[...] = jnp.zeros_like(arrived)

    for chunk in range(CHUNKS):

        @pl.when(above)
        def _():
            spill_copy(chunk).wait_recv()

        for tile in range(chunk * width, (chunk + 1) * width):
            for row in range(band_tiles):
                lines = slice(row * side, (row + 1) * side)
                total = own_ref[tile, lines, :] + arrived[tile, lines, :]
                out_ref[row, tile, me] = tiles_ref[row, tile] - step_size * total

        @pl.when(has_right)
        def _():
            rightward(me, 0, chunk).start()

        @pl.when(has_left)
        def _():
            leftward(me, 0, chunk).start()

    for step in range(1, groups):
        for chunk in range(CHUNKS):

            @pl.when(me >= step)
            def _():
                rightward(me - step, step - 1, chunk).wait_recv()

            if step < groups - 1:

                @pl.when((me >= step) & has_right)
                def _():
                    rightward(me - step, step, chunk).start()

            @pl.when(me + step < groups)
            def _():
                leftward(me + step, step - 1, chunk).wait_recv()

            if step < groups - 1:

                @pl.when((me + step < groups) & has_left)
                def _():
                    leftward(me + step, step, chunk).start()

    for chunk in range(CHUNKS):

        @pl.when(below)
        def _():
            spill_copy(chunk).wait_send()

        for step in range(groups - 1):

            @pl.when((me >= step) & has_right)
            def _():
                rightward(me - step, step, chunk).wait_send()

            @pl.when((me + step < groups) & has_left)
            def _():
                leftward(me + step, step, chunk).wait_send()


def finish(tiles, own, spill, groups, regions):
    band_tiles, across, side, _ = tiles.shape
    sems = pltpu.SemaphoreType.DMA((groups - 1, CHUNKS))
    return pl.pallas_call(
        functools.partial(finish_kernel, regions, groups),
        out_shape=jax.ShapeDtypeStruct((band_tiles, across, groups, side, side), jnp.float32),
        in_specs=[full_spec()] * 3,
        out_specs=full_spec(),
        scratch_shapes=[
            pltpu.VMEM(own.shape, jnp.float32),
            pltpu.SemaphoreType.DMA((CHUNKS,)),
            pltpu.SemaphoreType.DMA((CHUNKS,)),
            sems,
            sems,
            sems,
            sems,
        ],
        compiler_params=pltpu.CompilerParams(
            collective_id=0, has_side_effects=True, vmem_limit_bytes=32 * 1024 * 1024
        ),
    )(tiles, own, spill)


def dense_update(object_tiles, gradients, rows, columns, band_rows):
    _, slices, _, side, _ = object_tiles.shape
    components, pixels = gradients[0].shape[0], gradients[0].shape[1]
    band_tiles = band_rows // side
    canvas = jnp.zeros((components, 2 * band_rows, TGX * side), jnp.float32)
    zero = jnp.int32(0)
    for slot, gradient in enumerate(gradients):
        corner = (zero, rows[slot], columns[slot])
        former = lax.dynamic_slice(canvas, corner, gradient.shape)
        canvas = lax.dynamic_update_slice(canvas, former + gradient, corner)
    shaped = canvas.reshape(components, 2, band_tiles, side, TGX, side).transpose(1, 2, 4, 0, 3, 5)
    shaped = shaped.reshape(2, -1, side)
    combined = lax.psum(shaped[0] + shifted(shaped[1], "region", 1), "pos")
    return object_tiles - step_size * combined.reshape(object_tiles.shape)


def per_device(object_tiles, probe, fresnel_phase, patterns, row_offsets, col_offsets, counts):
    slots = patterns.shape[2]
    pixels = patterns.shape[-1]
    held, slices, _, side, _ = object_tiles.shape
    components = 2 * slices
    band_tiles = held // TGX
    band_rows = band_tiles * side
    groups = lax.axis_size("pos")
    me = lax.axis_index("pos")
    tiles = object_tiles.reshape(held, components, side, side)
    measured = patterns.reshape(slots, pixels, pixels)
    rows = row_offsets.reshape(slots) - lax.axis_index("region") * band_rows
    columns = col_offsets.reshape(slots)
    live = (jnp.arange(slots, dtype=jnp.int32) < counts.reshape(())).astype(jnp.int32)

    wanted = shifted(columns, "region", 1)
    windows = column_windows(wanted, tiles, pixels)
    halos = []
    for slot in range(slots):
        window = windows[slot]
        if halos:
            window, halos[-1] = lax.optimization_barrier((window, halos[-1]))
        halos.append(shifted(window, "region", -1))

    matrices = make_matrices(pixels)
    wave = jnp.stack([jnp.cos(fresnel_phase), jnp.sin(fresnel_phase)])
    places = jnp.stack([rows, columns, live], axis=1)

    gradients = [
        position_gradient(places[slot], tiles, halos[slot], probe, wave, measured[slot], matrices)
        for slot in range(slots)
    ]
    if groups != components:
        gradients = [gradient[:, :pixels] for gradient in gradients]
        return dense_update(object_tiles, gradients, rows, columns, band_rows)

    parts = []
    for gradient in gradients:
        for by in range(groups):
            piece = lax.dynamic_index_in_dim(gradient, lax.rem(me + by, groups), 0, keepdims=False)
            parts.append(piece if by == 0 else rotated(piece, "pos", by))
    own, spill = scatter(parts, band_rows)
    mine = lax.dynamic_index_in_dim(tiles, me, 1, keepdims=False)
    mine = mine.reshape(band_tiles, TGX, side, side)
    result = finish(mine, own, spill, groups, lax.axis_size("region"))
    return result.reshape(object_tiles.shape)


def solution(mesh):
    in_specs = (
        P("region", None, None, None, None),
        P(),
        P(),
        P("region", "pos", None, None, None),
        P("region", "pos", None),
        P("region", "pos", None),
        P("region", "pos"),
    )
    out_specs = P("region", None, None, None, None)
    return jax.shard_map(
        per_device, mesh=mesh, in_specs=in_specs, out_specs=out_specs, check_vma=False
    )
```
